512 devices in a mesh: space: 64 (over x, z, y_lo), ens: 8 (over y_hi, core).
Axes of the slice: x: 4, y: 8 (y_hi: 4, y_lo: 2; y = y_hi * 2 + y_lo), z: 8, core: 2. Of those that a mesh axis runs over, the one named last changes fastest.
Arguments:
- state: bfloat16 [8, 16, 1024, 384], P('ens', None, 'space'), may hold values from -6 to 6
- cotangent: bfloat16 [8, 16, 1024, 384], P('ens', None, 'space'), may hold values from -6 to 6
- halo_cols: int32 [16], replicated, may hold values from 1 to 16, as said below
- row_offset: int32 [16, 4], replicated, may hold values from -2 to 2
- conv_weight: float32 [4, 384], replicated, may hold values from -4 to 4
- norm_gain: float32 [384], replicated, may hold values from 0.5 to 1.5
- weight_in: bfloat16 [384, 768], replicated, may hold values from -0.3125 to 0.3125
- weight_out: bfloat16 [768, 384], replicated, may hold values from -0.21875 to 0.21875
Outputs:
- grad_state: bfloat16 [8, 16, 1024, 384], P('ens', None, 'space')
- grad_conv: float32 [4, 384], replicated
- grad_gain: float32 [384], replicated
- grad_in: bfloat16 [384, 768], replicated
- grad_out: bfloat16 [768, 384], replicated
The draws below stay inside these ranges and needn't reach their ends.
Inputs may be any that keep to these rules, and one draw needn't show every extreme that they name: halo_cols rises with the row index, within one of a straight rise from 1 at row 0 to 16 at the last row, which is the polar one.
All inputs are finite; a program needn't handle non-finite values.
Results may differ from the reference program's by a relative error of at most 0.0078.
Values may be sent and summed in bfloat16 or wider, within the bound.
No kernel may reach another device: no remote copies, remote signals or barrier semaphores. Data moves between devices by JAX's collectives and lax.ppermute only.
A program may use at most 64 MiB of HBM per device.

```python
import math
import jax
import jax.numpy as jnp
from jax import lax

C = 384
FF = 768
K = 4
HMAX = 16
ROWS = 16
MEMBERS = 8
NLON = 1024


def draw_halo_cols(key, part):
    key = jax.random.fold_in(key, 7)
    row_ids = jnp.arange(ROWS, dtype=jnp.int32)
    rising = 1 + row_ids * (HMAX - 1) // max(ROWS - 1, 1)
    jitter = jax.random.randint(key, (ROWS,), 0, 2, dtype=jnp.int32)
    widths = jnp.clip(rising - jitter, 1, HMAX)
    widths = widths.at[ROWS - 1].set(HMAX)
    widths = widths.at[0].set(1)
    return widths.astype(jnp.int32)


def plant(drawn, rng, smallest, top_value):
    spot = [jax.random.randint(jax.random.fold_in(rng, axis), (), 0, length) for axis, length in enumerate(drawn.shape)]
    widest = drawn.shape.index(max(drawn.shape))
    beside = spot[:widest] + [(spot[widest] + 1) % drawn.shape[widest]] + spot[widest + 1:]
    return drawn.at[tuple(spot)].set(smallest).at[tuple(beside)].set(top_value)


def block_scale(key, shape, pieces, low, high):
    def one(position, parts):
        draws = jax.random.uniform(jax.random.fold_in(jax.random.fold_in(key, 6), position), (parts,), jnp.float32, low / len(pieces), high / len(pieces))
        return jnp.repeat(jnp.exp(draws), shape[position] // parts).reshape((-1,) + (1,) * (len(shape) - position - 1))

    level = one(*pieces[0])
    for cut in pieces[1:]:
        level = level * one(*cut)
    return level


def noise(rng, shape, width, most, shards=(), kind=jnp.bfloat16):
    result = width * jax.random.normal(rng, shape, jnp.float32)
    if shards:
        result = result * block_scale(rng, shape, shards, -0.22, 0.18)
    return jnp.clip(result, -most, most).astype(kind)


def setup_inputs(seed: int = 0) -> dict:
    key_list = jax.random.split(jax.random.key(seed), 9)
    state = noise(key_list[0], (MEMBERS, ROWS, NLON, C), 1.0, 6.0, ((0, 8), (2, 64)))
    cotangent = noise(key_list[1], (MEMBERS, ROWS, NLON, C), 1.0, 6.0, ((0, 8), (2, 64)))
    halo_cols = draw_halo_cols(jax.random.fold_in(key_list[8], 71), 0)
    row_offset = plant(jax.random.randint(key_list[3], (ROWS, K), -2, 3), jax.random.fold_in(key_list[3], 1), -2, 2).astype(jnp.int32)
    conv_weight = noise(key_list[4], (K, C), 1.0, 4.0, (), jnp.float32)
    norm_gain = jnp.clip(1.0 + 0.1 * jax.random.normal(key_list[5], (C,), jnp.float32), 0.5, 1.5)
    weight_in = noise(key_list[6], (C, FF), C ** -0.5, 0.3125)
    weight_out = noise(key_list[7], (FF, C), FF ** -0.5, 0.21875)
    return {"state": state, "cotangent": cotangent, "halo_cols": halo_cols, "row_offset": row_offset, "conv_weight": conv_weight, "norm_gain": norm_gain, "weight_in": weight_in, "weight_out": weight_out}


norm_eps = 1e-05

def basis_profiles(halo_cols):
    steps_off = jnp.arange(2 * HMAX + 1, dtype=jnp.int32) - HMAX
    reach = halo_cols.astype(jnp.float32)[:, None]
    ratio = steps_off.astype(jnp.float32)[None, :] / (reach + 1.0)
    inside = jnp.abs(steps_off)[None, :] <= halo_cols[:, None]
    base = jnp.where(inside, (1.0 - ratio * ratio) / jnp.sqrt(reach + 1.0), jnp.zeros_like(ratio))
    return jnp.stack([base * ratio ** power for power in range(K)], axis=1).astype(jnp.bfloat16)

def conv_all(field, profile, row_offset):
    row_ids = jnp.arange(ROWS, dtype=jnp.int32)
    stacked = []
    for basis_id in range(K):
        source = (row_ids + row_offset[:, basis_id]).astype(jnp.int32)
        valid = (source >= 0) & (source < ROWS)
        picked = jnp.where(valid[:, None, None], field[jnp.clip(source, 0, ROWS - 1)], jnp.zeros_like(field))
        padded = jnp.concatenate([picked[:, NLON - HMAX:], picked, picked[:, :HMAX]], axis=1)
        weights = profile[:, basis_id].astype(jnp.float32)
        total = jnp.zeros_like(field)
        for entry in range(2 * HMAX + 1):
            total = total + weights[:, entry][:, None, None] * padded[:, entry:entry + NLON]
        stacked.append(total)
    return jnp.stack(stacked)

def reference(state, cotangent, halo_cols, row_offset, conv_weight, norm_gain, weight_in, weight_out):
    profile = basis_profiles(halo_cols)
    weights_f = conv_weight.astype(jnp.float32)

    def member(pair):
        one_state, one_grad = pair
        values = one_state.astype(jnp.float32)
        responses, adjoint = jax.vjp(lambda field: conv_all(field, profile, row_offset), values)
        filtered = lax.optimization_barrier(jnp.sum(weights_f[:, None, None, :] * responses, axis=0))
        flat_mixed = filtered.reshape(ROWS * NLON, C)
        center = lax.optimization_barrier(jnp.mean(flat_mixed, axis=-1, keepdims=True))
        offset_vals = flat_mixed - center
        variance = lax.optimization_barrier(jnp.mean(offset_vals * offset_vals, axis=-1, keepdims=True))
        inverse = 1.0 / jnp.sqrt(variance + norm_eps)
        normed = offset_vals * inverse
        scaled = (normed * norm_gain).astype(jnp.bfloat16)
        preact = jnp.dot(scaled, weight_in, preferred_element_type=jnp.float32)
        hidden_vals, gelu_back = jax.vjp(jax.nn.gelu, preact)
        hidden = hidden_vals.astype(jnp.bfloat16)
        flat_grad = one_grad.reshape(ROWS * NLON, C)
        out_term = jnp.dot(hidden.T, flat_grad, preferred_element_type=jnp.float32)
        grad_hidden = jnp.dot(flat_grad, weight_out.T, preferred_element_type=jnp.float32)
        grad_preact = gelu_back(grad_hidden)[0].astype(jnp.bfloat16)
        in_term = jnp.dot(scaled.T, grad_preact, preferred_element_type=jnp.float32)
        grad_scaled = jnp.dot(grad_preact, weight_in.T, preferred_element_type=jnp.float32)
        gain_term = lax.optimization_barrier(jnp.sum(grad_scaled * normed, axis=0))
        grad_normed = grad_scaled * norm_gain
        grad_filtered = (grad_normed - lax.optimization_barrier(jnp.mean(grad_normed, axis=-1, keepdims=True)) - normed * lax.optimization_barrier(jnp.mean(grad_normed * normed, axis=-1, keepdims=True))) * inverse
        grad_field = grad_filtered.reshape(ROWS, NLON, C)
        conv_term = lax.optimization_barrier(jnp.sum(grad_field[None] * responses, axis=(1, 2)))
        grad_rounded = grad_field.astype(jnp.bfloat16)
        back = adjoint(weights_f[:, None, None, :] * grad_rounded.astype(jnp.float32))[0]
        grad_one = (one_grad.astype(jnp.float32) + back).astype(jnp.bfloat16)
        return (grad_one, conv_term, gain_term, in_term, out_term)
    results = lax.map(member, (state, cotangent))
    factor = 1.0 / math.sqrt(MEMBERS * ROWS * NLON)
    grad_conv = lax.optimization_barrier(jnp.sum(results[1], axis=0)) * factor
    grad_gain = lax.optimization_barrier(jnp.sum(results[2], axis=0)) * factor
    grad_in = (lax.optimization_barrier(jnp.sum(results[3], axis=0)) * factor).astype(jnp.bfloat16)
    grad_out = (lax.optimization_barrier(jnp.sum(results[4], axis=0)) * factor).astype(jnp.bfloat16)
    return (results[0], grad_conv, grad_gain, grad_in, grad_out)
```

```python
import math

import jax
import jax.numpy as jnp
from jax import lax
from jax.sharding import Mesh, PartitionSpec as P

K = 4
HMAX = 16
REACH = 2
SPAN = 2 * REACH + 1
EXTRA = 8


norm_eps = 1e-05
f32 = jnp.float32
bf16 = jnp.bfloat16
SPACE = ("x", "z", "yl")
ENS = ("yh", "core")


def shifted(value, axes, by):
    count = lax.axis_size(axes)
    return lax.ppermute(value, axes, [(i, (i + by) % count) for i in range(count)])


def swap_cores(value):
    return lax.ppermute(value, "core", [(0, 1), (1, 0)])


def band_blocks(halo_cols, row_offset, row_count, col_count):
    padded = col_count + 2 * HMAX
    shape = (row_count, K * col_count, SPAN * padded)
    out_id = lax.broadcasted_iota(jnp.int32, shape, 1)
    src_id = lax.broadcasted_iota(jnp.int32, shape, 2)
    basis = out_id // col_count
    column = out_id % col_count
    source_row = src_id // padded - REACH
    step = src_id % padded - column - HMAX
    reach = halo_cols[:, None, None]
    ratio = step.astype(f32) / (reach.astype(f32) + 1.0)
    square = ratio * ratio
    power = jnp.where(basis == 0, 1.0, jnp.where(basis == 1, ratio, jnp.where(basis == 2, square, ratio * square)))
    value = (1.0 - square) / jnp.sqrt(reach.astype(f32) + 1.0) * power
    chosen = jnp.repeat(row_offset, col_count, axis=1)[:, :, None] == source_row
    inside = (jnp.abs(step) <= reach) & chosen
    return jnp.where(inside, value, 0.0).astype(bf16)


def split_pair(value):
    high = lax.reduce_precision(value, 8, 7)
    low = lax.reduce_precision(value - high, 8, 7)
    return high, low


def exchange(blocks, axes):
    return lax.all_to_all(blocks, axes, 0, 0, tiled=True)


def with_extras(blocks, extras):
    high, low = split_pair(extras)
    pair = jnp.concatenate([high, low], axis=0).astype(bf16)
    wide = jnp.broadcast_to(pair[None], (blocks.shape[0],) + pair.shape)
    return jnp.concatenate([blocks, wide], axis=1)


def summed(received, rows):
    total = jnp.sum(received.astype(f32), axis=0)
    return total[:rows], total[rows : rows + EXTRA] + total[rows + EXTRA :]


def reduce_all(in_term, out_term, extras, factor):
    core = lax.axis_index("core")
    rows, channels = in_term.shape
    mine = jnp.where(core == 0, in_term, out_term)
    theirs = jnp.where(core == 0, out_term, in_term).astype(bf16)
    high, low = split_pair(extras)
    got = swap_cores(jnp.concatenate([theirs, high.astype(bf16), low.astype(bf16)], axis=0)).astype(f32)
    mine = mine + got[:rows]
    extras = (high + low) + (got[rows : rows + EXTRA] + got[rows + EXTRA :])
    for axes in (("x", "yl"), ("yh",)):
        count = lax.axis_size(axes)
        rows = rows // count
        blocks = mine.astype(bf16).reshape(count, rows, channels)
        mine, extras = summed(exchange(with_extras(blocks, extras), axes), rows)
    count = lax.axis_size("z")
    blocks = jnp.broadcast_to(mine.astype(bf16)[None], (count, rows, channels))
    mine, extras = summed(exchange(with_extras(blocks, extras), "z"), rows)
    mine = (mine * factor).astype(bf16)
    for axes in (("yh",), ("x", "yl")):
        count = lax.axis_size(axes)
        blocks = jnp.broadcast_to(mine[None], (count, rows, channels))
        rows = rows * count
        mine = exchange(blocks, axes).reshape(rows, channels)
    other = swap_cores(mine)
    return jnp.where(core == 0, mine, other), jnp.where(core == 0, other, mine), extras * factor


def contract_cells(left, right):
    return lax.dot_general(left, right, (((0,), (0,)), ((), ())), preferred_element_type=f32)


def contract_features(left, right):
    return lax.dot_general(left, right, (((1,), (1,)), ((), ())), preferred_element_type=f32)


def on_device(state, cotangent, halo_cols, row_offset, conv_weight, norm_gain, weight_in, weight_out):
    local_state = state[0]
    local_grad = cotangent[0]
    row_count, col_count, channels = local_state.shape
    padded = col_count + 2 * HMAX
    west = shifted(local_state[:, col_count - HMAX :], SPACE, 1)
    east = shifted(local_state[:, :HMAX], SPACE, -1)
    bands = band_blocks(halo_cols, row_offset, row_count, col_count)
    extended = jnp.pad(
        jnp.concatenate([west, local_state, east], axis=1), ((REACH, REACH), (0, 0), (0, 0))
    )
    windows = jnp.stack(
        [extended[r : r + SPAN].reshape(SPAN * padded, channels) for r in range(row_count)]
    )
    responses = jnp.einsum("rmw,rwc->rmc", bands, windows, preferred_element_type=f32)
    responses = responses.reshape(row_count, K, col_count, channels)
    filtered = jnp.sum(conv_weight[None, :, None, :] * responses, axis=1)
    cell_count = row_count * col_count
    flat_mixed = filtered.reshape(cell_count, channels)
    center = jnp.mean(flat_mixed, axis=-1, keepdims=True)
    offset_vals = flat_mixed - center
    variance = jnp.mean(offset_vals * offset_vals, axis=-1, keepdims=True)
    inverse = 1.0 / jnp.sqrt(variance + norm_eps)
    normed = offset_vals * inverse
    scaled = (normed * norm_gain).astype(bf16)
    preact = jnp.dot(scaled, weight_in, preferred_element_type=f32)
    hidden_vals, gelu_back = jax.vjp(jax.nn.gelu, preact)
    hidden = hidden_vals.astype(bf16)
    flat_grad = local_grad.reshape(cell_count, channels)
    factor = 1.0 / math.sqrt(lax.axis_size(ENS) * cell_count * lax.axis_size(SPACE))
    out_term = contract_cells(hidden, flat_grad)
    grad_hidden = contract_features(flat_grad, weight_out)
    grad_preact = gelu_back(grad_hidden)[0].astype(bf16)
    half = grad_preact.shape[1] // 2
    in_term = jnp.concatenate(
        [contract_cells(scaled, grad_preact[:, :half]), contract_cells(scaled, grad_preact[:, half:])], axis=0
    )
    grad_scaled = contract_features(grad_preact, weight_in)
    gain_term = jnp.sum(grad_scaled * normed, axis=0)
    grad_normed = grad_scaled * norm_gain
    grad_filtered = (
        grad_normed
        - jnp.mean(grad_normed, axis=-1, keepdims=True)
        - normed * jnp.mean(grad_normed * normed, axis=-1, keepdims=True)
    ) * inverse
    grad_field = grad_filtered.reshape(row_count, col_count, channels)
    conv_term = jnp.sum(grad_field[:, None] * responses, axis=(0, 2))
    grad_rounded = grad_field.astype(bf16).astype(f32)
    weighted = (conv_weight[None, :, None, :] * grad_rounded[:, None]).astype(bf16)
    weighted = weighted.reshape(row_count, K * col_count, channels)
    parts = jnp.einsum("rmw,rmc->rwc", bands, weighted, preferred_element_type=f32)
    parts = parts.reshape(row_count, SPAN, padded, channels)
    spread_out = jnp.zeros((row_count, padded, channels), f32)
    for at in range(SPAN):
        by = at - REACH
        low, high = max(0, -by), row_count - max(0, by)
        spread_out = spread_out + jnp.pad(
            parts[low:high, at], ((max(0, by), max(0, -by)), (0, 0), (0, 0))
        )
    from_east = shifted(spread_out[:, :HMAX].astype(bf16), SPACE, -1).astype(f32)
    from_west = shifted(spread_out[:, col_count + HMAX :].astype(bf16), SPACE, 1).astype(f32)
    interior = spread_out[:, HMAX : HMAX + col_count]
    interior = interior.at[:, :HMAX].add(from_west)
    interior = interior.at[:, col_count - HMAX :].add(from_east)
    grad_state = (local_grad.astype(f32) + interior).astype(bf16)[None]
    extras = jnp.concatenate(
        [conv_term, gain_term[None], jnp.zeros((EXTRA - K - 1, channels), f32)], axis=0
    )
    in_total, grad_out, extra_total = reduce_all(in_term, out_term, extras, factor)
    grad_in = jnp.concatenate([in_total[:channels], in_total[channels:]], axis=1)
    return (grad_state, extra_total[:K], extra_total[K], grad_in, grad_out)


def solution(mesh):
    fine = Mesh(mesh.devices.reshape(4, 8, 2, 4, 2), SPACE + ENS)
    field = P(ENS, None, SPACE, None)
    return jax.shard_map(
        on_device,
        mesh=fine,
        in_specs=(field, field, P(), P(), P(), P(), P(), P()),
        out_specs=(field, P(), P(), P(), P()),
        check_vma=False,
    )
```

```python
import math

import jax
import jax.numpy as jnp
from jax import lax
from jax.sharding import Mesh, PartitionSpec as P

K = 4
HMAX = 16
REACH = 2
SPAN = 2 * REACH + 1
EXTRA = 8


norm_eps = 1e-05
f32 = jnp.float32
bf16 = jnp.bfloat16
SPACE = ("x", "z", "yl")
ENS = ("yh", "core")


def shifted(value, axes, by):
    count = lax.axis_size(axes)
    return lax.ppermute(value, axes, [(i, (i + by) % count) for i in range(count)])


def swap_cores(value):
    return lax.ppermute(value, "core", [(0, 1), (1, 0)])


def band_blocks(halo_cols, row_offset, row_count, col_count):
    padded = col_count + 2 * HMAX
    shape = (row_count, K * col_count, SPAN * padded)
    out_id = lax.broadcasted_iota(jnp.int32, shape, 1)
    src_id = lax.broadcasted_iota(jnp.int32, shape, 2)
    basis = out_id // col_count
    column = out_id % col_count
    source_row = src_id // padded - REACH
    step = src_id % padded - column - HMAX
    reach = halo_cols[:, None, None]
    ratio = step.astype(f32) / (reach.astype(f32) + 1.0)
    square = ratio * ratio
    power = jnp.where(basis == 0, 1.0, jnp.where(basis == 1, ratio, jnp.where(basis == 2, square, ratio * square)))
    value = (1.0 - square) / jnp.sqrt(reach.astype(f32) + 1.0) * power
    chosen = jnp.repeat(row_offset, col_count, axis=1)[:, :, None] == source_row
    inside = (jnp.abs(step) <= reach) & chosen
    return jnp.where(inside, value, 0.0).astype(bf16)


def rounded(value):
    return lax.reduce_precision(value, 8, 7)


def exchange(blocks, axes):
    return lax.all_to_all(blocks, axes, 0, 0, tiled=True)


def with_extras(blocks, extras):
    wide = jnp.broadcast_to(extras.astype(bf16)[None], (blocks.shape[0],) + extras.shape)
    return jnp.concatenate([blocks, wide], axis=1)


def summed(received, rows):
    total = jnp.sum(received.astype(f32), axis=0)
    return total[:rows], total[rows:]


def copies(value, count):
    return jnp.broadcast_to(value[None], (count,) + value.shape)


def reduce_all(in_term, out_term, extras, factor, beside):
    seed, adjoint, send, finish = beside
    core = lax.axis_index("core")
    channels = extras.shape[1]
    first = jnp.concatenate([in_term[0], out_term[:channels]], axis=0)
    second = jnp.concatenate([in_term[1], out_term[channels:]], axis=0)
    rows = 2 * channels
    mine = jnp.where(core == 0, first, second)
    theirs = jnp.where(core == 0, second, first).astype(bf16)
    extras = rounded(extras)
    got = swap_cores(jnp.concatenate([theirs, extras.astype(bf16)], axis=0)).astype(f32)
    mine = mine + got[:rows]
    extras = extras + got[rows:]
    rows = rows // 8
    blocks = with_extras(mine.astype(bf16).reshape(8, rows, channels), extras)
    blocks, seed = lax.optimization_barrier((blocks, seed))
    work = adjoint(seed)
    got, work = lax.optimization_barrier((exchange(blocks, ("x", "yl")), work))
    mine, extras = summed(got, rows)
    rows = rows // 4
    blocks = with_extras(mine.astype(bf16).reshape(4, rows, channels), extras)
    mine, extras = summed(exchange(blocks, ("yh",)), rows)
    blocks = copies(jnp.concatenate([mine, extras], axis=0).astype(bf16), 8)
    blocks, edges = lax.optimization_barrier((blocks, work[:2]))
    sent = send(edges)
    total = jnp.sum(exchange(blocks, ("z",)).astype(f32), axis=0) * factor
    blocks = copies(total[:rows].astype(bf16), 4)
    rows = rows * 4
    mine = exchange(blocks, ("yh",)).reshape(rows, channels)
    blocks, sent = lax.optimization_barrier((copies(mine, 8), sent))
    rows = rows * 8
    mine = exchange(blocks, ("x", "yl")).reshape(rows, channels)
    mine, sent, work, total = lax.optimization_barrier((mine, sent, work, total))
    other = swap_cores(mine)
    done = finish(work, sent)
    first = jnp.where(core == 0, mine, other)
    second = jnp.where(core == 0, other, mine)
    grad_in = jnp.concatenate([first[:channels], second[:channels]], axis=1)
    grad_out = jnp.concatenate([first[channels:], second[channels:]], axis=0)
    return grad_in, grad_out, total[total.shape[0] - EXTRA :], done


def contract_cells(left, right):
    return lax.dot_general(left, right, (((0,), (0,)), ((), ())), preferred_element_type=f32)


def contract_features(left, right):
    return lax.dot_general(left, right, (((1,), (1,)), ((), ())), preferred_element_type=f32)


def on_device(state, cotangent, halo_cols, row_offset, conv_weight, norm_gain, weight_in, weight_out):
    local_state = state[0]
    local_grad = cotangent[0]
    row_count, col_count, channels = local_state.shape
    padded = col_count + 2 * HMAX
    west = shifted(local_state[:, col_count - HMAX :], SPACE, 1)
    east = shifted(local_state[:, :HMAX], SPACE, -1)
    bands = band_blocks(halo_cols, row_offset, row_count, col_count)
    extended = jnp.pad(
        jnp.concatenate([west, local_state, east], axis=1), ((REACH, REACH), (0, 0), (0, 0))
    )
    windows = jnp.stack(
        [extended[r : r + SPAN].reshape(SPAN * padded, channels) for r in range(row_count)]
    )
    responses = jnp.einsum("rmw,rwc->rmc", bands, windows, preferred_element_type=f32)
    responses = responses.reshape(row_count, K, col_count, channels)
    filtered = jnp.sum(conv_weight[None, :, None, :] * responses, axis=1)
    cell_count = row_count * col_count
    flat_mixed = filtered.reshape(cell_count, channels)
    center = jnp.mean(flat_mixed, axis=-1, keepdims=True)
    offset_vals = flat_mixed - center
    variance = jnp.mean(offset_vals * offset_vals, axis=-1, keepdims=True)
    inverse = 1.0 / jnp.sqrt(variance + norm_eps)
    normed = offset_vals * inverse
    scaled = (normed * norm_gain).astype(bf16)
    preact = jnp.dot(scaled, weight_in, preferred_element_type=f32)
    hidden_vals, gelu_back = jax.vjp(jax.nn.gelu, preact)
    hidden = hidden_vals.astype(bf16)
    flat_grad = local_grad.reshape(cell_count, channels)
    factor = 1.0 / math.sqrt(lax.axis_size(ENS) * cell_count * lax.axis_size(SPACE))
    out_term = contract_cells(hidden, flat_grad)
    grad_hidden = contract_features(flat_grad, weight_out)
    grad_preact = gelu_back(grad_hidden)[0].astype(bf16)
    half = grad_preact.shape[1] // 2
    in_term = contract_cells(scaled, grad_preact[:, :half]), contract_cells(scaled, grad_preact[:, half:])
    grad_scaled = contract_features(grad_preact, weight_in)
    gain_term = jnp.sum(grad_scaled * normed, axis=0)
    grad_normed = grad_scaled * norm_gain
    grad_filtered = (
        grad_normed
        - jnp.mean(grad_normed, axis=-1, keepdims=True)
        - normed * jnp.mean(grad_normed * normed, axis=-1, keepdims=True)
    ) * inverse
    grad_field = grad_filtered.reshape(row_count, col_count, channels)
    conv_term = jnp.sum(grad_field[:, None] * responses, axis=(0, 2))

    def adjoint(grad_rounded):
        grad_rounded = grad_rounded.astype(f32)
        weighted = (conv_weight[None, :, None, :] * grad_rounded[:, None]).astype(bf16)
        weighted = weighted.reshape(row_count, K * col_count, channels)
        parts = jnp.einsum("rmw,rmc->rwc", bands, weighted, preferred_element_type=f32)
        parts = parts.reshape(row_count, SPAN, padded, channels)
        spread_out = jnp.zeros((row_count, padded, channels), f32)
        for at in range(SPAN):
            by = at - REACH
            low, high = max(0, -by), row_count - max(0, by)
            spread_out = spread_out + jnp.pad(
                parts[low:high, at], ((max(0, by), max(0, -by)), (0, 0), (0, 0))
            )
        return (
            spread_out[:, :HMAX].astype(bf16),
            spread_out[:, col_count + HMAX :].astype(bf16),
            local_grad.astype(f32) + spread_out[:, HMAX : HMAX + col_count],
        )

    def send(work):
        return shifted(work[0], SPACE, -1), shifted(work[1], SPACE, 1)

    def finish(work, sent):
        interior = work[2]
        from_east, from_west = sent[0].astype(f32), sent[1].astype(f32)
        interior = interior.at[:, :HMAX].add(from_west)
        interior = interior.at[:, col_count - HMAX :].add(from_east)
        return interior.astype(bf16)[None]

    extras = jnp.concatenate(
        [conv_term, gain_term[None], jnp.zeros((EXTRA - K - 1, channels), f32)], axis=0
    )
    grad_in, grad_out, extra_total, grad_state = reduce_all(
        in_term, out_term, extras, factor, (grad_field.astype(bf16), adjoint, send, finish)
    )
    return (grad_state, extra_total[:K], extra_total[K], grad_in, grad_out)


def solution(mesh):
    fine = Mesh(mesh.devices.reshape(4, 8, 2, 4, 2), SPACE + ENS)
    field = P(ENS, None, SPACE, None)
    return jax.shard_map(
        on_device,
        mesh=fine,
        in_specs=(field, field, P(), P(), P(), P(), P(), P()),
        out_specs=(field, P(), P(), P(), P()),
        check_vma=False,
    )
```

```python
import math

import jax
import jax.numpy as jnp
from jax import lax
from jax.experimental import pallas as pl
from jax.experimental.pallas import tpu as pltpu
from jax.sharding import Mesh, PartitionSpec as P

K = 4
HMAX = 16
REACH = 2
SPAN = 2 * REACH + 1
EXTRA = 8


norm_eps = 1e-05
f32 = jnp.float32
bf16 = jnp.bfloat16
SPACE = ("x", "z", "yl")
ENS = ("yh", "core")


def shifted(value, axes, by):
    count = lax.axis_size(axes)
    return lax.ppermute(value, axes, [(i, (i + by) % count) for i in range(count)])


def swap_cores(value):
    return lax.ppermute(value, "core", [(0, 1), (1, 0)])


def band_blocks(halo_cols, row_offset, row_count, col_count):
    padded = col_count + 2 * HMAX
    shape = (row_count, K * col_count, SPAN * padded)
    out_id = lax.broadcasted_iota(jnp.int32, shape, 1)
    src_id = lax.broadcasted_iota(jnp.int32, shape, 2)
    basis = out_id // col_count
    column = out_id % col_count
    source_row = src_id // padded - REACH
    step = src_id % padded - column - HMAX
    reach = halo_cols[:, None, None]
    ratio = step.astype(f32) / (reach.astype(f32) + 1.0)
    square = ratio * ratio
    power = jnp.where(basis == 0, 1.0, jnp.where(basis == 1, ratio, jnp.where(basis == 2, square, ratio * square)))
    value = (1.0 - square) / jnp.sqrt(reach.astype(f32) + 1.0) * power
    chosen = jnp.repeat(row_offset, col_count, axis=1)[:, :, None] == source_row
    inside = (jnp.abs(step) <= reach) & chosen
    return jnp.where(inside, value, 0.0).astype(bf16)


def rounded(value):
    return lax.reduce_precision(value, 8, 7)


def exchange(blocks, axes):
    return lax.all_to_all(blocks, axes, 0, 0, tiled=True)


def with_extras(blocks, extras):
    wide = jnp.broadcast_to(extras.astype(bf16)[None], (blocks.shape[0],) + extras.shape)
    return jnp.concatenate([blocks, wide], axis=1)


def summed(received, rows):
    total = jnp.sum(received.astype(f32), axis=0)
    return total[:rows], total[rows:]


def copies(value, count):
    return jnp.broadcast_to(value[None], (count,) + value.shape)


def reduce_all(mine, theirs, extras, factor, beside):
    seed, adjoint, send, finish = beside
    core = lax.axis_index("core")
    rows, channels = mine.shape
    got = swap_cores(theirs).astype(f32)
    mine = mine + got[:rows]
    extras = rounded(extras) + got[rows : rows + EXTRA]
    rows = rows // 8
    blocks = with_extras(mine.astype(bf16).reshape(8, rows, channels), extras)
    blocks, seed = lax.optimization_barrier((blocks, seed))
    work = adjoint(seed)
    got, work = lax.optimization_barrier((exchange(blocks, ("x", "yl")), work))
    mine, extras = summed(got, rows)
    rows = rows // 4
    blocks = with_extras(mine.astype(bf16).reshape(4, rows, channels), extras)
    mine, extras = summed(exchange(blocks, ("yh",)), rows)
    blocks = copies(jnp.concatenate([mine, extras], axis=0).astype(bf16), 8)
    blocks, edges = lax.optimization_barrier((blocks, work[:2]))
    sent = send(edges)
    total = jnp.sum(exchange(blocks, ("z",)).astype(f32), axis=0) * factor
    blocks = copies(total[:rows].astype(bf16), 4)
    rows = rows * 4
    mine = exchange(blocks, ("yh",)).reshape(rows, channels)
    at = total.shape[0] - EXTRA
    blocks, sent, grad_conv, grad_gain = lax.optimization_barrier(
        (copies(mine, 8), sent, total[at : at + K], total[at + K])
    )
    rows = rows * 8
    mine = exchange(blocks, ("x", "yl")).reshape(rows, channels)
    mine, sent, work = lax.optimization_barrier((mine, sent, work))
    other = swap_cores(mine)
    done = finish(work, sent)
    first = jnp.where(core == 0, mine, other)
    second = jnp.where(core == 0, other, mine)
    grad_in = jnp.concatenate([first[:channels], second[:channels]], axis=1)
    grad_out = jnp.concatenate([first[channels:], second[channels:]], axis=0)
    return done, grad_conv, grad_gain, grad_in, grad_out


def contract_cells(left, right):
    return lax.dot_general(left, right, (((0,), (0,)), ((), ())), preferred_element_type=f32)


def contract_features(left, right):
    return lax.dot_general(left, right, (((1,), (1,)), ((), ())), preferred_element_type=f32)


def gelu_pair(value):
    slope = math.sqrt(2.0 / math.pi)
    square = value * value
    bend = jnp.tanh(slope * value * (1.0 + 0.044715 * square))
    gate = 0.5 * (1.0 + bend)
    back = gate + 0.5 * value * (1.0 - bend * bend) * (slope * (1.0 + 3.0 * 0.044715 * square))
    return value * gate, back


def block_kernel(
    core_ref, ext_ref, bands_ref, hid_grad_ref, vec_ref, cot_hbm, win_hbm,
    mine_ref, theirs_ref, extras_ref, grad_ref,
    cot_ref, win_ref, resp, filt, hid, back, sems,
):
    row_count = bands_ref.shape[0]
    col_count = bands_ref.shape[1] // K
    channels = ext_ref.shape[1]
    padded = col_count + 2 * HMAX
    load_win = pltpu.make_async_copy(win_hbm, win_ref, sems.at[0])
    load_cot = pltpu.make_async_copy(cot_hbm, cot_ref, sems.at[1])
    load_win.start()
    load_cot.start()
    for r in range(row_count):
        y = jnp.dot(bands_ref[r], ext_ref[r * padded : (r + SPAN) * padded], preferred_element_type=f32)
        resp[r] = y
        mixed = vec_ref[0:1] * y[:col_count]
        for k in range(1, K):
            mixed = mixed + vec_ref[k : k + 1] * y[k * col_count : (k + 1) * col_count]
        filt[r * col_count : (r + 1) * col_count] = mixed
    flat = filt[...]
    center = jnp.mean(flat, axis=-1, keepdims=True)
    offset = flat - center
    variance = jnp.mean(offset * offset, axis=-1, keepdims=True)
    inverse = 1.0 / jnp.sqrt(variance + norm_eps)
    normed = offset * inverse
    gain = vec_ref[K : K + 1]
    scaled = (normed * gain).astype(bf16)
    load_win.wait()
    preact = jnp.dot(scaled, win_ref[...], preferred_element_type=f32)
    hidden, slope = gelu_pair(preact)
    hid[...] = hidden.astype(bf16)
    grad_preact = (hid_grad_ref[...] * slope).astype(bf16)
    back[...] = grad_preact
    grad_scaled = contract_features(grad_preact, win_ref[...])
    load_cot.wait()
    cot = cot_ref[...]
    own = pl.multiple_of(core_ref[0] * channels, 128)
    other = pl.multiple_of((1 - core_ref[0]) * channels, 128)
    mine_ref[:channels] = contract_cells(scaled, back[:, pl.ds(own, channels)])
    mine_ref[channels:] = contract_cells(hid[:, pl.ds(own, channels)], cot)
    theirs_ref[:channels] = contract_cells(scaled, back[:, pl.ds(other, channels)]).astype(bf16)
    theirs_ref[channels : 2 * channels] = contract_cells(hid[:, pl.ds(other, channels)], cot).astype(bf16)
    gain_term = jnp.sum(grad_scaled * normed, axis=0, keepdims=True)
    grad_normed = grad_scaled * gain
    grad = (
        grad_normed
        - jnp.mean(grad_normed, axis=-1, keepdims=True)
        - normed * jnp.mean(grad_normed * normed, axis=-1, keepdims=True)
    ) * inverse
    grad_ref[...] = grad.astype(bf16)
    filt[...] = grad
    sums = [jnp.zeros((col_count, channels), f32)] * K
    for r in range(row_count):
        piece = filt[r * col_count : (r + 1) * col_count]
        for k in range(K):
            sums[k] = sums[k] + piece * resp[r, k * col_count : (k + 1) * col_count]
    extras = jnp.concatenate(
        [jnp.sum(part, axis=0, keepdims=True) for part in sums]
        + [gain_term, jnp.zeros((2 * EXTRA - K - 1, channels), f32)],
        axis=0,
    )
    extras_ref[...] = extras[:EXTRA]
    theirs_ref[2 * channels :] = extras.astype(bf16)


def block(extended, bands, hidden_grad, vectors, cotangent, weight_in):
    row_count = bands.shape[0]
    col_count = bands.shape[1] // K
    cells = row_count * col_count
    channels, wide = weight_in.shape
    vmem = pl.BlockSpec(memory_space=pltpu.VMEM)
    core = lax.axis_index("core").astype(jnp.int32)[None]
    return pl.pallas_call(
        block_kernel,
        out_shape=(
            jax.ShapeDtypeStruct((2 * channels, channels), f32),
            jax.ShapeDtypeStruct((2 * channels + 2 * EXTRA, channels), bf16),
            jax.ShapeDtypeStruct((EXTRA, channels), f32),
            jax.ShapeDtypeStruct((cells, channels), bf16),
        ),
        in_specs=[pl.BlockSpec(memory_space=pltpu.SMEM)] + [vmem] * 4 + [pl.BlockSpec(memory_space=pl.ANY)] * 2,
        out_specs=(vmem,) * 4,
        scratch_shapes=[
            pltpu.VMEM((cells, channels), bf16),
            pltpu.VMEM((channels, wide), bf16),
            pltpu.VMEM((row_count, K * col_count, channels), f32),
            pltpu.VMEM((cells, channels), f32),
            pltpu.VMEM((cells, wide), bf16),
            pltpu.VMEM((cells, wide), bf16),
            pltpu.SemaphoreType.DMA((2,)),
        ],
        compiler_params=pltpu.CompilerParams(vmem_limit_bytes=32 * 1024 * 1024),
        cost_estimate=pl.CostEstimate(
            flops=10 * cells * channels * wide, bytes_accessed=4 * channels * wide, transcendentals=cells * wide
        ),
    )(core, extended, bands, hidden_grad, vectors, cotangent, weight_in)


def on_device(state, cotangent, halo_cols, row_offset, conv_weight, norm_gain, weight_in, weight_out):
    local_state = state[0]
    local_grad = cotangent[0]
    row_count, col_count, channels = local_state.shape
    padded = col_count + 2 * HMAX
    west = shifted(local_state[:, col_count - HMAX :], SPACE, 1)
    east = shifted(local_state[:, :HMAX], SPACE, -1)
    bands = band_blocks(halo_cols, row_offset, row_count, col_count)
    cell_count = row_count * col_count
    factor = 1.0 / math.sqrt(lax.axis_size(ENS) * cell_count * lax.axis_size(SPACE))
    flat_grad = local_grad.reshape(cell_count, channels)
    extended = jnp.concatenate([west, local_state, east], axis=1)
    extended = jnp.pad(extended, ((REACH, REACH), (0, 0), (0, 0))).reshape(-1, channels)
    vectors = jnp.concatenate([conv_weight, norm_gain[None], jnp.zeros((8 - K - 1, channels), f32)], axis=0)
    mine, theirs, extras, grad_field = block(
        extended, bands, contract_features(flat_grad, weight_out), vectors, flat_grad, weight_in
    )

    def adjoint(grad_rounded):
        grad_rounded = grad_rounded.astype(f32).reshape(row_count, col_count, channels)
        weighted = (conv_weight[None, :, None, :] * grad_rounded[:, None]).astype(bf16)
        weighted = weighted.reshape(row_count, K * col_count, channels)
        parts = jnp.einsum("rmw,rmc->rwc", bands, weighted, preferred_element_type=f32)
        parts = parts.reshape(row_count, SPAN, padded, channels)
        spread_out = jnp.zeros((row_count, padded, channels), f32)
        for at in range(SPAN):
            by = at - REACH
            low, high = max(0, -by), row_count - max(0, by)
            spread_out = spread_out + jnp.pad(
                parts[low:high, at], ((max(0, by), max(0, -by)), (0, 0), (0, 0))
            )
        return (
            spread_out[:, :HMAX].astype(bf16),
            spread_out[:, col_count + HMAX :].astype(bf16),
            local_grad.astype(f32) + spread_out[:, HMAX : HMAX + col_count],
        )

    def send(work):
        return shifted(work[0], SPACE, -1), shifted(work[1], SPACE, 1)

    def finish(work, sent):
        interior = work[2]
        from_east, from_west = sent[0].astype(f32), sent[1].astype(f32)
        interior = interior.at[:, :HMAX].add(from_west)
        interior = interior.at[:, col_count - HMAX :].add(from_east)
        return interior.astype(bf16)[None]

    return reduce_all(mine, theirs, extras, factor, (grad_field, adjoint, send, finish))


def solution(mesh):
    fine = Mesh(mesh.devices.reshape(4, 8, 2, 4, 2), SPACE + ENS)
    field = P(ENS, None, SPACE, None)
    return jax.shard_map(
        on_device,
        mesh=fine,
        in_specs=(field, field, P(), P(), P(), P(), P(), P()),
        out_specs=(field, P(), P(), P(), P()),
        check_vma=False,
    )
```

```python
import math

import jax
import jax.numpy as jnp
from jax import lax
from jax.experimental import pallas as pl
from jax.experimental.pallas import tpu as pltpu
from jax.sharding import Mesh, PartitionSpec as P

K = 4
HMAX = 16
REACH = 2
SPAN = 2 * REACH + 1
EXTRA = 8


norm_eps = 1e-05
f32 = jnp.float32
bf16 = jnp.bfloat16
SPACE = ("x", "z", "yl")
ENS = ("yh", "core")


def shifted(value, axes, by):
    count = lax.axis_size(axes)
    return lax.ppermute(value, axes, [(i, (i + by) % count) for i in range(count)])


def swap_cores(value):
    return lax.ppermute(value, "core", [(0, 1), (1, 0)])


def band_blocks(halo_cols, row_offset, row_count, col_count):
    padded = col_count + 2 * HMAX
    shape = (row_count, K * col_count, SPAN * padded)
    out_id = lax.broadcasted_iota(jnp.int32, shape, 1)
    src_id = lax.broadcasted_iota(jnp.int32, shape, 2)
    basis = out_id // col_count
    column = out_id % col_count
    source_row = src_id // padded - REACH
    step = src_id % padded - column - HMAX
    reach = halo_cols[:, None, None]
    ratio = step.astype(f32) / (reach.astype(f32) + 1.0)
    square = ratio * ratio
    power = jnp.where(basis == 0, 1.0, jnp.where(basis == 1, ratio, jnp.where(basis == 2, square, ratio * square)))
    value = (1.0 - square) / jnp.sqrt(reach.astype(f32) + 1.0) * power
    chosen = jnp.repeat(row_offset, col_count, axis=1)[:, :, None] == source_row
    inside = (jnp.abs(step) <= reach) & chosen
    return jnp.where(inside, value, 0.0).astype(bf16)


def rounded(value):
    return lax.reduce_precision(value, 8, 7)


def exchange(blocks, axes):
    return lax.all_to_all(blocks, axes, 0, 0, tiled=True)


def with_extras(blocks, extras):
    wide = jnp.broadcast_to(extras.astype(bf16)[None], (blocks.shape[0],) + extras.shape)
    return jnp.concatenate([blocks, wide], axis=1)


def summed(received, rows):
    total = jnp.sum(received.astype(f32), axis=0)
    return total[:rows], total[rows:]


def copies(value, count):
    return jnp.broadcast_to(value[None], (count,) + value.shape)


def reduce_all(mine, theirs, extras, factor, beside):
    seed, adjoint, send, finish = beside
    core = lax.axis_index("core")
    rows, channels = mine.shape
    got = swap_cores(theirs).astype(f32)
    mine = mine + got[:rows]
    extras = rounded(extras) + got[rows : rows + EXTRA]
    rows = rows // 8
    blocks = with_extras(mine.astype(bf16).reshape(8, rows, channels), extras)
    blocks, seed = lax.optimization_barrier((blocks, seed))
    work = adjoint(seed)
    got, work = lax.optimization_barrier((exchange(blocks, ("x", "yl")), work))
    mine, extras = summed(got, rows)
    rows = rows // 4
    blocks = with_extras(mine.astype(bf16).reshape(4, rows, channels), extras)
    mine, extras = summed(exchange(blocks, ("yh",)), rows)
    blocks = copies(jnp.concatenate([mine, extras], axis=0).astype(bf16), 8)
    blocks, edges = lax.optimization_barrier((blocks, work[:2]))
    sent = send(edges)
    total = jnp.sum(exchange(blocks, ("z",)).astype(f32), axis=0) * factor
    blocks, total = lax.optimization_barrier((copies(total[:rows].astype(bf16), 4), total))
    small = total[rows : rows + K], total[rows + K]
    rows = rows * 4
    mine = exchange(blocks, ("yh",)).reshape(rows, channels)
    blocks, sent, small = lax.optimization_barrier((copies(mine, 8), sent, small))
    rows = rows * 8
    mine = exchange(blocks, ("x", "yl")).reshape(rows, channels)
    mine, sent, work = lax.optimization_barrier((mine, sent, work))
    other = swap_cores(mine)
    done = finish(work, sent)
    first = jnp.where(core == 0, mine[:channels], other[:channels])
    second = jnp.where(core == 0, other[:channels], mine[:channels])
    grad_in = jnp.concatenate([first, second], axis=1)
    halves = jnp.zeros((2, channels, channels), bf16)
    halves = lax.dynamic_update_index_in_dim(halves, mine[channels:], core, 0)
    halves = lax.dynamic_update_index_in_dim(halves, other[channels:], 1 - core, 0)
    grad_out = halves.reshape(2 * channels, channels)
    grad_conv, grad_gain = small
    return done, grad_conv, grad_gain, grad_in, grad_out


def contract_cells(left, right):
    return lax.dot_general(left, right, (((0,), (0,)), ((), ())), preferred_element_type=f32)


def contract_features(left, right):
    return lax.dot_general(left, right, (((1,), (1,)), ((), ())), preferred_element_type=f32)


def gelu_pair(value):
    slope = math.sqrt(2.0 / math.pi)
    square = value * value
    bend = jnp.tanh(slope * value * (1.0 + 0.044715 * square))
    gate = 0.5 * (1.0 + bend)
    back = gate + 0.5 * value * (1.0 - bend * bend) * (slope * (1.0 + 3.0 * 0.044715 * square))
    return value * gate, back


def block_kernel(
    core_ref, ext_ref, bands_ref, hid_grad_ref, vec_ref, cot_hbm, win_hbm,
    mine_ref, theirs_ref, extras_ref, grad_ref,
    cot_ref, win_ref, resp, filt, hid, back, sems,
):
    row_count = bands_ref.shape[0]
    col_count = bands_ref.shape[1] // K
    channels = ext_ref.shape[1]
    padded = col_count + 2 * HMAX
    load_win = pltpu.make_async_copy(win_hbm, win_ref, sems.at[0])
    load_cot = pltpu.make_async_copy(cot_hbm, cot_ref, sems.at[1])
    load_win.start()
    load_cot.start()
    for r in range(row_count):
        y = jnp.dot(bands_ref[r], ext_ref[r * padded : (r + SPAN) * padded], preferred_element_type=f32)
        resp[r] = y
        mixed = vec_ref[0:1] * y[:col_count]
        for k in range(1, K):
            mixed = mixed + vec_ref[k : k + 1] * y[k * col_count : (k + 1) * col_count]
        filt[r * col_count : (r + 1) * col_count] = mixed
    flat = filt[...]
    center = jnp.mean(flat, axis=-1, keepdims=True)
    offset = flat - center
    variance = jnp.mean(offset * offset, axis=-1, keepdims=True)
    inverse = 1.0 / jnp.sqrt(variance + norm_eps)
    normed = offset * inverse
    gain = vec_ref[K : K + 1]
    scaled = (normed * gain).astype(bf16)
    load_win.wait()
    preact = jnp.dot(scaled, win_ref[...], preferred_element_type=f32)
    hidden, slope = gelu_pair(preact)
    hid[...] = hidden.astype(bf16)
    grad_preact = (hid_grad_ref[...] * slope).astype(bf16)
    back[...] = grad_preact
    grad_scaled = contract_features(grad_preact, win_ref[...])
    load_cot.wait()
    cot = cot_ref[...]
    own = pl.multiple_of(core_ref[0] * channels, 128)
    other = pl.multiple_of((1 - core_ref[0]) * channels, 128)
    mine_ref[:channels] = contract_cells(scaled, back[:, pl.ds(own, channels)])
    mine_ref[channels:] = contract_cells(hid[:, pl.ds(own, channels)], cot)
    theirs_ref[:channels] = contract_cells(scaled, back[:, pl.ds(other, channels)]).astype(bf16)
    theirs_ref[channels : 2 * channels] = contract_cells(hid[:, pl.ds(other, channels)], cot).astype(bf16)
    gain_term = jnp.sum(grad_scaled * normed, axis=0, keepdims=True)
    grad_normed = grad_scaled * gain
    grad = (
        grad_normed
        - jnp.mean(grad_normed, axis=-1, keepdims=True)
        - normed * jnp.mean(grad_normed * normed, axis=-1, keepdims=True)
    ) * inverse
    grad_ref[...] = grad.astype(bf16)
    filt[...] = grad
    sums = [jnp.zeros((col_count, channels), f32)] * K
    for r in range(row_count):
        piece = filt[r * col_count : (r + 1) * col_count]
        for k in range(K):
            sums[k] = sums[k] + piece * resp[r, k * col_count : (k + 1) * col_count]
    extras = jnp.concatenate(
        [jnp.sum(part, axis=0, keepdims=True) for part in sums]
        + [gain_term, jnp.zeros((2 * EXTRA - K - 1, channels), f32)],
        axis=0,
    )
    extras_ref[...] = extras[:EXTRA]
    theirs_ref[2 * channels :] = extras.astype(bf16)


def block(extended, bands, hidden_grad, vectors, cotangent, weight_in):
    row_count = bands.shape[0]
    col_count = bands.shape[1] // K
    cells = row_count * col_count
    channels, wide = weight_in.shape
    vmem = pl.BlockSpec(memory_space=pltpu.VMEM)
    core = lax.axis_index("core").astype(jnp.int32)[None]
    return pl.pallas_call(
        block_kernel,
        out_shape=(
            jax.ShapeDtypeStruct((2 * channels, channels), f32),
            jax.ShapeDtypeStruct((2 * channels + 2 * EXTRA, channels), bf16),
            jax.ShapeDtypeStruct((EXTRA, channels), f32),
            jax.ShapeDtypeStruct((cells, channels), bf16),
        ),
        in_specs=[pl.BlockSpec(memory_space=pltpu.SMEM)] + [vmem] * 4 + [pl.BlockSpec(memory_space=pl.ANY)] * 2,
        out_specs=(vmem,) * 4,
        scratch_shapes=[
            pltpu.VMEM((cells, channels), bf16),
            pltpu.VMEM((channels, wide), bf16),
            pltpu.VMEM((row_count, K * col_count, channels), f32),
            pltpu.VMEM((cells, channels), f32),
            pltpu.VMEM((cells, wide), bf16),
            pltpu.VMEM((cells, wide), bf16),
            pltpu.SemaphoreType.DMA((2,)),
        ],
        compiler_params=pltpu.CompilerParams(vmem_limit_bytes=32 * 1024 * 1024),
        cost_estimate=pl.CostEstimate(
            flops=10 * cells * channels * wide, bytes_accessed=4 * channels * wide, transcendentals=cells * wide
        ),
    )(core, extended, bands, hidden_grad, vectors, cotangent, weight_in)


def on_device(state, cotangent, halo_cols, row_offset, conv_weight, norm_gain, weight_in, weight_out):
    local_state = state[0]
    local_grad = cotangent[0]
    row_count, col_count, channels = local_state.shape
    padded = col_count + 2 * HMAX
    west = shifted(local_state[:, col_count - HMAX :], SPACE, 1)
    east = shifted(local_state[:, :HMAX], SPACE, -1)
    bands = band_blocks(halo_cols, row_offset, row_count, col_count)
    cell_count = row_count * col_count
    factor = 1.0 / math.sqrt(lax.axis_size(ENS) * cell_count * lax.axis_size(SPACE))
    flat_grad = local_grad.reshape(cell_count, channels)
    extended = jnp.concatenate([west, local_state, east], axis=1)
    extended = jnp.pad(extended, ((REACH, REACH), (0, 0), (0, 0))).reshape(-1, channels)
    vectors = jnp.concatenate([conv_weight, norm_gain[None], jnp.zeros((8 - K - 1, channels), f32)], axis=0)
    mine, theirs, extras, grad_field = block(
        extended, bands, contract_features(flat_grad, weight_out), vectors, flat_grad, weight_in
    )

    def adjoint(grad_rounded):
        grad_rounded = grad_rounded.astype(f32).reshape(row_count, col_count, channels)
        weighted = (conv_weight[None, :, None, :] * grad_rounded[:, None]).astype(bf16)
        weighted = weighted.reshape(row_count, K * col_count, channels)
        parts = jnp.einsum("rmw,rmc->rwc", bands, weighted, preferred_element_type=f32)
        parts = parts.reshape(row_count, SPAN, padded, channels)
        spread_out = jnp.zeros((row_count, padded, channels), f32)
        for at in range(SPAN):
            by = at - REACH
            low, high = max(0, -by), row_count - max(0, by)
            spread_out = spread_out + jnp.pad(
                parts[low:high, at], ((max(0, by), max(0, -by)), (0, 0), (0, 0))
            )
        return (
            spread_out[:, :HMAX].astype(bf16),
            spread_out[:, col_count + HMAX :].astype(bf16),
            local_grad.astype(f32) + spread_out[:, HMAX : HMAX + col_count],
        )

    def send(work):
        return shifted(work[0], SPACE, -1), shifted(work[1], SPACE, 1)

    def finish(work, sent):
        interior = work[2]
        from_east, from_west = sent[0].astype(f32), sent[1].astype(f32)
        interior = interior.at[:, :HMAX].add(from_west)
        interior = interior.at[:, col_count - HMAX :].add(from_east)
        return interior.astype(bf16)[None]

    return reduce_all(mine, theirs, extras, factor, (grad_field, adjoint, send, finish))


def solution(mesh):
    fine = Mesh(mesh.devices.reshape(4, 8, 2, 4, 2), SPACE + ENS)
    field = P(ENS, None, SPACE, None)
    return jax.shard_map(
        on_device,
        mesh=fine,
        in_specs=(field, field, P(), P(), P(), P(), P(), P()),
        out_specs=(field, P(), P(), P(), P()),
        check_vma=False,
    )
```
